512 devices in a mesh: tm: 16 (over y, core), clus: 32 (over z, x).
Axes of the slice: x: 4, y: 8, z: 8, core: 2. Of those that a mesh axis runs over, the one named last changes fastest.
Arguments:
- series: bfloat16 [65536, 1024], P(('clus', 'tm')), parts along dimension 0, may hold values from -11 to 11
- block_time: int32 [1024], P('clus'), parts along dimension 0, may hold values from 0 to 31, each once
- w_qkv: bfloat16 [1024, 3072], replicated, may hold values from -0.1875 to 0.1875
- w_out: bfloat16 [1024, 1024], replicated, may hold values from -0.1875 to 0.1875
Outputs:
- result: bfloat16 [65536, 1024], P(('clus', 'tm')), parts along dimension 0
The draws below stay inside these ranges and needn't reach their ends.
There are 32 independent parts, one for each index of `clus`. The reference program is written for one: setup_inputs(seed, part) draws one part's arguments, and reference() takes and returns one part's arrays. A program takes and returns all parts, laid end to end along the dimension named above; an argument that names none is the same for every part. Nothing has to cross between parts.
Inputs may be any that keep to these rules, and one draw needn't show every extreme that they name: block_time is a permutation of the stored blocks' time indices.
All inputs are finite; a program needn't handle non-finite values.
Results may differ from the reference program's by a relative error of at most 0.012.
The reference program's roundings to bfloat16 on the way (of `qkv`, `probs` and `attended`) count: a program that leaves them out, or rounds other values in their place, can miss the bound.
Values may be sent and summed in bfloat16 or wider, within the bound.
No kernel may reach another device: no remote copies, remote signals or barrier semaphores. Data moves between devices by JAX's collectives and lax.ppermute only.
A program may use at most 128 MiB of HBM per device.

```python
import jax
import jax.numpy as jnp
from jax import lax

HEADS = 16
HEAD = 64
D = 1024
TOK_DEV = 128
BLK = 64
TOKENS = 2048
N_TM = 16


def draw_series(key, part):
    key = jax.random.fold_in(key, 7)
    first = jax.random.fold_in(key, 0)
    values = jnp.clip(jax.random.normal(first, (TOKENS, D), jnp.float32), -6.0, 6.0)
    return values.astype(jnp.bfloat16)


def scatter_about(key, dims, scale, bound, kind=jnp.bfloat16):
    array = jax.random.normal(key, dims, jnp.float32) * scale
    return jnp.minimum(jnp.maximum(array, -bound), bound).astype(kind)


def setup_inputs(seed: int = 0, part: int = 0) -> dict:
    seeds = jax.random.split(jax.random.key(seed), 5)
    part_keys = jax.random.split(jax.random.fold_in(seeds[4], part), 5)
    return {
        "series": draw_series(jax.random.fold_in(jax.random.fold_in(seeds[4], part), 71), part),
        "block_time": jax.random.permutation(part_keys[1], 2 * N_TM).astype(jnp.int32),
        "w_qkv": scatter_about(seeds[2], (D, 3 * D), D ** -0.5, 0.1875),
        "w_out": scatter_about(seeds[3], (D, D), D ** -0.5, 0.1875),
    }


def reference(series, block_time, w_qkv, w_out):
    qkv = jnp.dot(series, w_qkv, preferred_element_type=jnp.float32).astype(jnp.bfloat16)
    times = (block_time[:, None] * BLK + jnp.arange(BLK, dtype=jnp.int32)[None, :]).reshape(-1).astype(jnp.int32)
    queries = qkv[:, :D].reshape(N_TM, TOK_DEV, HEADS, HEAD)
    keys = qkv[:, D:2 * D].reshape(TOKENS, HEADS, HEAD).astype(jnp.float32)
    values = qkv[:, 2 * D:].reshape(TOKENS, HEADS, HEAD).astype(jnp.float32)
    qtimes = times.reshape(N_TM, TOK_DEV)

    def one_block(item):
        block, qtime = item
        scores = jnp.einsum("lhe,mhe->hlm", block.astype(jnp.float32), keys) * 0.125
        keep = times[None, None, :] <= qtime[None, :, None]
        top = jnp.max(jnp.where(keep, scores, -1e30), axis=-1)
        probs = jnp.where(keep, jnp.exp(scores - top[:, :, None]), 0.0)
        total = jnp.sum(probs, axis=-1)
        rounded = probs.astype(jnp.bfloat16).astype(jnp.float32)
        summed = jnp.einsum("hlm,mhe->lhe", rounded, values)
        return (summed / total.T[:, :, None]).reshape(TOK_DEV, D).astype(jnp.bfloat16)

    attended = lax.map(one_block, (queries, qtimes)).reshape(TOKENS, D)
    mixed = series.astype(jnp.float32) + jnp.dot(attended, w_out, preferred_element_type=jnp.float32)
    return mixed.astype(jnp.bfloat16)
```

```python
import jax
import jax.numpy as jnp
from jax import lax
from jax.experimental import pallas as pl
from jax.experimental.pallas import tpu as pltpu
from jax.sharding import PartitionSpec as P

HEADS = 16
HEAD = 64
D = 1024
BLK = 64
ROWS = 2 * BLK
N_TM = 16
TOKENS = N_TM * ROWS
TILE = 256
GROUP = 256
NT = (((1,), (1,)), ((), ()))
SCALE = 0.125 * 1.4426950408889634


def swap_halves(tile):
    top, low = tile[:BLK], tile[BLK:]
    first = jnp.concatenate([top[:, :HEAD], low[:, :HEAD]], axis=1)
    second = jnp.concatenate([top[:, HEAD:], low[:, HEAD:]], axis=1)
    return first, second


def project_kernel(x_ref, w_ref, out_ref, w_buf, sem):
    groups = D // GROUP
    copies = []
    for g in range(groups):
        for part in range(3):
            columns = pl.ds(part * D + g * GROUP, GROUP)
            copy = pltpu.make_async_copy(
                w_ref.at[:, columns], w_buf.at[g * 3 + part], sem.at[g * 3 + part]
            )
            copy.start()
            copies.append(copy)
    x = x_ref[...]
    for g in range(groups):
        for part in range(3):
            copies[g * 3 + part].wait()
            y = jnp.dot(x, w_buf[g * 3 + part], preferred_element_type=jnp.float32)
            y = y.astype(jnp.bfloat16)
            for pair in range(GROUP // 128):
                first, second = swap_halves(y[:, pair * 128 : pair * 128 + 128])
                head = g * (GROUP // HEAD) + 2 * pair
                out_ref[head, part * BLK : part * BLK + BLK, :] = first
                out_ref[head + 1, part * BLK : part * BLK + BLK, :] = second


def project(x, w):
    return pl.pallas_call(
        project_kernel,
        out_shape=jax.ShapeDtypeStruct((HEADS, 3 * BLK, ROWS), jnp.bfloat16),
        in_specs=[
            pl.BlockSpec(memory_space=pltpu.VMEM),
            pl.BlockSpec(memory_space=pl.ANY),
        ],
        out_specs=pl.BlockSpec(memory_space=pltpu.VMEM),
        scratch_shapes=[
            pltpu.VMEM((3 * D // GROUP, D, GROUP), jnp.bfloat16),
            pltpu.SemaphoreType.DMA((3 * D // GROUP,)),
        ],
        compiler_params=pltpu.CompilerParams(vmem_limit_bytes=56 * 2**20),
        name="project",
    )(x, w)


def attend_kernel(time_ref, in_ref, out_ref, qs, ks, vs, vt, os):
    for b in range(2 * N_TM):
        source, half = b // 2, b % 2
        rows = pl.ds(pl.multiple_of(time_ref[b] * BLK, BLK), BLK)
        for part, ref in enumerate((qs, ks, vs)):
            ref[rows, :] = in_ref[
                source, part * BLK : part * BLK + BLK, half * HEAD : half * HEAD + HEAD
            ]
    for i in range(TOKENS // TILE):
        span = slice(i * TILE, (i + 1) * TILE)
        vt[:, span] = vs[span, :].T
    before = lax.broadcasted_iota(jnp.int32, (TILE, TILE), 0)
    after = lax.broadcasted_iota(jnp.int32, (TILE, TILE), 1)
    keep = before <= after
    for i in range(TOKENS // TILE):
        span = slice(i * TILE, (i + 1) * TILE)
        q = qs[span, :]
        diagonal = lax.dot_general(ks[span, :], q, NT, preferred_element_type=jnp.float32)
        diagonal = jnp.where(keep, diagonal, -1e30)
        tops = jnp.max(diagonal, axis=0, keepdims=True)
        if i:
            scores = lax.dot_general(
                ks[: i * TILE, :], q, NT, preferred_element_type=jnp.float32
            )
            tops = jnp.maximum(tops, jnp.max(scores, axis=0, keepdims=True))
        probs = jnp.exp2((diagonal - tops) * SCALE)
        total = jnp.sum(probs, axis=0, keepdims=True)
        summed = jnp.dot(
            vt[:, span], probs.astype(jnp.bfloat16), preferred_element_type=jnp.float32
        )
        if i:
            probs = jnp.exp2((scores - tops) * SCALE)
            total = total + jnp.sum(probs, axis=0, keepdims=True)
            summed = summed + jnp.dot(
                vt[:, : i * TILE], probs.astype(jnp.bfloat16), preferred_element_type=jnp.float32
            )
        os[span, :] = (summed / total).astype(jnp.bfloat16).T
    for s in range(N_TM):
        pair = []
        for half in range(2):
            rows = pl.ds(pl.multiple_of(time_ref[2 * s + half] * BLK, BLK), BLK)
            pair.append(os[rows, :])
        out_ref[s] = jnp.concatenate(pair, axis=1)


def attend(block_time, received):
    return pl.pallas_call(
        attend_kernel,
        out_shape=jax.ShapeDtypeStruct((N_TM, BLK, ROWS), jnp.bfloat16),
        in_specs=[
            pl.BlockSpec(memory_space=pltpu.SMEM),
            pl.BlockSpec(memory_space=pltpu.VMEM),
        ],
        out_specs=pl.BlockSpec(memory_space=pltpu.VMEM),
        scratch_shapes=[pltpu.VMEM((TOKENS, HEAD), jnp.bfloat16)] * 3
        + [pltpu.VMEM((HEAD, TOKENS), jnp.bfloat16), pltpu.VMEM((TOKENS, HEAD), jnp.bfloat16)],
        compiler_params=pltpu.CompilerParams(vmem_limit_bytes=32 * 2**20),
        name="attend",
    )(block_time, received)


def mix_kernel(in_ref, x_ref, w_ref, out_ref, rows_ref):
    for pair in range(HEADS // 2):
        first, second = in_ref[2 * pair], in_ref[2 * pair + 1]
        columns = slice(pair * 128, pair * 128 + 128)
        rows_ref[:BLK, columns] = jnp.concatenate([first[:, :HEAD], second[:, :HEAD]], axis=1)
        rows_ref[BLK:, columns] = jnp.concatenate([first[:, HEAD:], second[:, HEAD:]], axis=1)
    mixed = jnp.dot(rows_ref[...], w_ref[...], preferred_element_type=jnp.float32)
    out_ref[...] = (x_ref[...].astype(jnp.float32) + mixed).astype(jnp.bfloat16)


def mix(attended, x, w):
    return pl.pallas_call(
        mix_kernel,
        out_shape=jax.ShapeDtypeStruct((ROWS, D), jnp.bfloat16),
        in_specs=[pl.BlockSpec(memory_space=pltpu.VMEM)] * 3,
        out_specs=pl.BlockSpec(memory_space=pltpu.VMEM),
        scratch_shapes=[pltpu.VMEM((ROWS, D), jnp.bfloat16)],
        compiler_params=pltpu.CompilerParams(vmem_limit_bytes=16 * 2**20),
        name="mix",
    )(attended, x, w)


def shards(series, block_time, w_qkv, w_out):
    sent = project(series, w_qkv)
    received = lax.all_to_all(sent, "tm", 0, 0, tiled=True)
    attended = attend(block_time, received)
    returned = lax.all_to_all(attended, "tm", 0, 0, tiled=True)
    return mix(returned, series, w_out)


def solution(mesh):
    placed = (P(("clus", "tm"), None), P("clus"), P(), P())
    return jax.shard_map(
        shards, mesh=mesh, in_specs=placed, out_specs=P(("clus", "tm"), None), check_vma=False
    )
```

```python
import jax
import jax.numpy as jnp
from jax import lax
from jax.experimental import pallas as pl
from jax.experimental.pallas import tpu as pltpu
from jax.sharding import PartitionSpec as P

HEADS = 16
HEAD = 64
D = 1024
BLK = 64
ROWS = 2 * BLK
N_TM = 16
TOKENS = N_TM * ROWS
QTILE = 512
KTILE = 1024
GROUP = 256
CHUNK = 256
PROJECT_VMEM = 52 * 2**20
NT = (((1,), (1,)), ((), ()))
SCALE = 0.125 * 1.4426950408889634


def swap_halves(tile):
    top, low = tile[:BLK], tile[BLK:]
    first = jnp.concatenate([top[:, :HEAD], low[:, :HEAD]], axis=1)
    second = jnp.concatenate([top[:, HEAD:], low[:, HEAD:]], axis=1)
    return first, second


def project_kernel(x_ref, w_ref, out_ref, w_buf, total, sem):
    chunks = D // CHUNK
    copies = []
    for c in range(chunks):
        rows = pl.ds(c * CHUNK, CHUNK)
        copies.append(pltpu.make_async_copy(w_ref.at[rows], w_buf.at[rows], sem.at[c]))
        copies[-1].start()
    for c in range(chunks):
        copies[c].wait()
        depth = slice(c * CHUNK, (c + 1) * CHUNK)
        for g in range(3 * D // GROUP):
            columns = slice(g * GROUP, (g + 1) * GROUP)
            y = jnp.dot(
                x_ref[:, depth], w_buf[depth, columns], preferred_element_type=jnp.float32
            )
            if c:
                y = y + total[:, columns]
            if c < chunks - 1:
                total[:, columns] = y
                continue
            y = y.astype(jnp.bfloat16)
            part, start = g * GROUP // D, g * GROUP % D
            for pair in range(GROUP // 128):
                first, second = swap_halves(y[:, pair * 128 : pair * 128 + 128])
                head = start // HEAD + 2 * pair
                out_ref[head, part * BLK : part * BLK + BLK, :] = first
                out_ref[head + 1, part * BLK : part * BLK + BLK, :] = second


def project(x, w):
    return pl.pallas_call(
        project_kernel,
        out_shape=jax.ShapeDtypeStruct((HEADS, 3 * BLK, ROWS), jnp.bfloat16),
        in_specs=[
            pl.BlockSpec(memory_space=pltpu.VMEM),
            pl.BlockSpec(memory_space=pl.ANY),
        ],
        out_specs=pl.BlockSpec(memory_space=pltpu.VMEM),
        scratch_shapes=[
            pltpu.VMEM((D, 3 * D), jnp.bfloat16),
            pltpu.VMEM((ROWS, 3 * D), jnp.float32),
            pltpu.SemaphoreType.DMA((D // CHUNK,)),
        ],
        compiler_params=pltpu.CompilerParams(vmem_limit_bytes=PROJECT_VMEM),
        name="project",
    )(x, w)


def attend_kernel(time_ref, in_ref, out_ref, qs, ks, vs, os):
    ones = jnp.ones((BLK, HEAD), jnp.bfloat16)
    for b in range(2 * N_TM):
        source, half = b // 2, b % 2
        rows = pl.ds(pl.multiple_of(time_ref[b] * BLK, BLK), BLK)
        columns = slice(half * HEAD, half * HEAD + HEAD)
        qs[rows, :] = in_ref[source, :BLK, columns]
        ks[rows, :] = in_ref[source, BLK : 2 * BLK, columns]
        vs[rows, :] = jnp.concatenate([in_ref[source, 2 * BLK :, columns], ones], axis=1)
    for start in range(0, TOKENS, QTILE):
        q = qs[start : start + QTILE, :]
        top = summed = None
        for first in range(0, start + QTILE, KTILE):
            last = min(first + KTILE, start + QTILE)
            scores = lax.dot_general(q, ks[first:last, :], NT, preferred_element_type=jnp.float32)
            if last > start:
                shape = (QTILE, last - first)
                later = lax.broadcasted_iota(jnp.int32, shape, 0) + start
                earlier = lax.broadcasted_iota(jnp.int32, shape, 1) + first
                scores = jnp.where(earlier <= later, scores, -1e30)
            new_top = jnp.max(scores, axis=1, keepdims=True)
            if top is not None:
                new_top = jnp.maximum(top, new_top)
            probs = jnp.exp2((scores - new_top) * SCALE).astype(jnp.bfloat16)
            added = jnp.dot(probs, vs[first:last, :], preferred_element_type=jnp.float32)
            if top is not None:
                added = summed * jnp.exp2((top - new_top) * SCALE) + added
            top, summed = new_top, added
        os[start : start + QTILE, :] = (summed[:, :HEAD] / summed[:, HEAD:]).astype(jnp.bfloat16)
    for s in range(N_TM):
        pair = []
        for half in range(2):
            rows = pl.ds(pl.multiple_of(time_ref[2 * s + half] * BLK, BLK), BLK)
            pair.append(os[rows, :])
        out_ref[s] = jnp.concatenate(pair, axis=1)


def attend(block_time, received):
    return pl.pallas_call(
        attend_kernel,
        out_shape=jax.ShapeDtypeStruct((N_TM, BLK, ROWS), jnp.bfloat16),
        in_specs=[
            pl.BlockSpec(memory_space=pltpu.SMEM),
            pl.BlockSpec(memory_space=pltpu.VMEM),
        ],
        out_specs=pl.BlockSpec(memory_space=pltpu.VMEM),
        scratch_shapes=[
            pltpu.VMEM((TOKENS, HEAD), jnp.bfloat16),
            pltpu.VMEM((TOKENS, HEAD), jnp.bfloat16),
            pltpu.VMEM((TOKENS, 2 * HEAD), jnp.bfloat16),
            pltpu.VMEM((TOKENS, HEAD), jnp.bfloat16),
        ],
        compiler_params=pltpu.CompilerParams(vmem_limit_bytes=32 * 2**20),
        name="attend",
    )(block_time, received)


def mix_kernel(in_ref, x_ref, w_ref, out_ref, rows_ref):
    for pair in range(HEADS // 2):
        first, second = in_ref[2 * pair], in_ref[2 * pair + 1]
        columns = slice(pair * 128, pair * 128 + 128)
        rows_ref[:BLK, columns] = jnp.concatenate([first[:, :HEAD], second[:, :HEAD]], axis=1)
        rows_ref[BLK:, columns] = jnp.concatenate([first[:, HEAD:], second[:, HEAD:]], axis=1)
    mixed = jnp.dot(rows_ref[...], w_ref[...], preferred_element_type=jnp.float32)
    out_ref[...] = (x_ref[...].astype(jnp.float32) + mixed).astype(jnp.bfloat16)


def mix(attended, x, w):
    return pl.pallas_call(
        mix_kernel,
        out_shape=jax.ShapeDtypeStruct((ROWS, D), jnp.bfloat16),
        in_specs=[pl.BlockSpec(memory_space=pltpu.VMEM)] * 3,
        out_specs=pl.BlockSpec(memory_space=pltpu.VMEM),
        scratch_shapes=[pltpu.VMEM((ROWS, D), jnp.bfloat16)],
        compiler_params=pltpu.CompilerParams(vmem_limit_bytes=16 * 2**20),
        name="mix",
    )(attended, x, w)


def shards(series, block_time, w_qkv, w_out):
    sent = project(series, w_qkv)
    sent, w_out = lax.optimization_barrier((sent, w_out))
    received = lax.all_to_all(sent, "tm", 0, 0, tiled=True)
    attended = attend(block_time, received)
    returned = lax.all_to_all(attended, "tm", 0, 0, tiled=True)
    return mix(returned, series, w_out)


def solution(mesh):
    placed = (P(("clus", "tm"), None), P("clus"), P(), P())
    return jax.shard_map(
        shards, mesh=mesh, in_specs=placed, out_specs=P(("clus", "tm"), None), check_vma=False
    )
```

```python
import jax
import jax.numpy as jnp
from jax import lax
from jax.experimental import pallas as pl
from jax.experimental.pallas import tpu as pltpu
from jax.sharding import PartitionSpec as P

HEADS = 16
HEAD = 64
D = 1024
BLK = 64
ROWS = 2 * BLK
N_TM = 16
TOKENS = N_TM * ROWS
QTILE = 512
KTILE = 1024
GROUP = 256
CHUNK = 256
PROJECT_VMEM = 24 * 2**20
NT = (((1,), (1,)), ((), ()))
SCALE = 0.125 * 1.4426950408889634


def in_hbm(array):
    return pltpu.with_memory_space_constraint(array, pltpu.HBM)


def in_vmem(array):
    return pltpu.with_memory_space_constraint(array, pltpu.VMEM)


def swap_halves(tile):
    top, low = tile[:BLK], tile[BLK:]
    first = jnp.concatenate([top[:, :HEAD], low[:, :HEAD]], axis=1)
    second = jnp.concatenate([top[:, HEAD:], low[:, HEAD:]], axis=1)
    return first, second


def project_kernel(x_ref, w_ref, out_ref, x_buf, w_buf, total, sem):
    chunks = D // CHUNK
    x_copy = pltpu.make_async_copy(x_ref, x_buf, sem.at[chunks])
    x_copy.start()
    copies = []
    for c in range(chunks):
        rows = pl.ds(c * CHUNK, CHUNK)
        copies.append(pltpu.make_async_copy(w_ref.at[rows], w_buf.at[rows], sem.at[c]))
        copies[-1].start()
    x_copy.wait()
    for c in range(chunks):
        copies[c].wait()
        depth = slice(c * CHUNK, (c + 1) * CHUNK)
        for g in range(3 * D // GROUP):
            columns = slice(g * GROUP, (g + 1) * GROUP)
            y = jnp.dot(
                x_buf[:, depth], w_buf[depth, columns], preferred_element_type=jnp.float32
            )
            if c:
                y = y + total[:, columns]
            if c < chunks - 1:
                total[:, columns] = y
                continue
            y = y.astype(jnp.bfloat16)
            part, start = g * GROUP // D, g * GROUP % D
            for pair in range(GROUP // 128):
                first, second = swap_halves(y[:, pair * 128 : pair * 128 + 128])
                head = start // HEAD + 2 * pair
                out_ref[head, part * BLK : part * BLK + BLK, :] = first
                out_ref[head + 1, part * BLK : part * BLK + BLK, :] = second


def project(x, w):
    return pl.pallas_call(
        project_kernel,
        out_shape=pltpu.VMEM((HEADS, 3 * BLK, ROWS), jnp.bfloat16),
        in_specs=[pl.BlockSpec(memory_space=pl.ANY)] * 2,
        out_specs=pl.BlockSpec(memory_space=pltpu.VMEM),
        scratch_shapes=[
            pltpu.VMEM((ROWS, D), jnp.bfloat16),
            pltpu.VMEM((D, 3 * D), jnp.bfloat16),
            pltpu.VMEM((ROWS, 3 * D), jnp.float32),
            pltpu.SemaphoreType.DMA((D // CHUNK + 1,)),
        ],
        compiler_params=pltpu.CompilerParams(vmem_limit_bytes=PROJECT_VMEM),
        name="project",
    )(in_hbm(x), in_hbm(w))


def attend_kernel(time_ref, in_ref, out_ref, qs, ks, vs, os):
    ones = jnp.ones((BLK, HEAD), jnp.bfloat16)
    for b in range(2 * N_TM):
        source, half = b // 2, b % 2
        rows = pl.ds(pl.multiple_of(time_ref[b] * BLK, BLK), BLK)
        columns = slice(half * HEAD, half * HEAD + HEAD)
        qs[rows, :] = in_ref[source, :BLK, columns]
        ks[rows, :] = in_ref[source, BLK : 2 * BLK, columns]
        vs[rows, :] = jnp.concatenate([in_ref[source, 2 * BLK :, columns], ones], axis=1)
    for start in range(0, TOKENS, QTILE):
        q = qs[start : start + QTILE, :]
        top = summed = None
        for first in range(0, start + QTILE, KTILE):
            last = min(first + KTILE, start + QTILE)
            scores = lax.dot_general(q, ks[first:last, :], NT, preferred_element_type=jnp.float32)
            if last > start:
                shape = (QTILE, last - first)
                later = lax.broadcasted_iota(jnp.int32, shape, 0) + start
                earlier = lax.broadcasted_iota(jnp.int32, shape, 1) + first
                scores = jnp.where(earlier <= later, scores, -1e30)
            new_top = jnp.max(scores, axis=1, keepdims=True)
            if top is not None:
                new_top = jnp.maximum(top, new_top)
            probs = jnp.exp2((scores - new_top) * SCALE).astype(jnp.bfloat16)
            added = jnp.dot(probs, vs[first:last, :], preferred_element_type=jnp.float32)
            if top is not None:
                added = summed * jnp.exp2((top - new_top) * SCALE) + added
            top, summed = new_top, added
        os[start : start + QTILE, :] = (summed[:, :HEAD] / summed[:, HEAD:]).astype(jnp.bfloat16)
    for s in range(N_TM):
        pair = []
        for half in range(2):
            rows = pl.ds(pl.multiple_of(time_ref[2 * s + half] * BLK, BLK), BLK)
            pair.append(os[rows, :])
        out_ref[s] = jnp.concatenate(pair, axis=1)


def attend(block_time, received):
    return pl.pallas_call(
        attend_kernel,
        out_shape=pltpu.VMEM((N_TM, BLK, ROWS), jnp.bfloat16),
        in_specs=[
            pl.BlockSpec(memory_space=pltpu.SMEM),
            pl.BlockSpec(memory_space=pltpu.VMEM),
        ],
        out_specs=pl.BlockSpec(memory_space=pltpu.VMEM),
        scratch_shapes=[
            pltpu.VMEM((TOKENS, HEAD), jnp.bfloat16),
            pltpu.VMEM((TOKENS, HEAD), jnp.bfloat16),
            pltpu.VMEM((TOKENS, 2 * HEAD), jnp.bfloat16),
            pltpu.VMEM((TOKENS, HEAD), jnp.bfloat16),
        ],
        compiler_params=pltpu.CompilerParams(vmem_limit_bytes=32 * 2**20),
        name="attend",
    )(block_time, in_vmem(received))


def mix_kernel(in_ref, x_ref, w_ref, out_ref, rows_ref):
    for pair in range(HEADS // 2):
        first, second = in_ref[2 * pair], in_ref[2 * pair + 1]
        columns = slice(pair * 128, pair * 128 + 128)
        rows_ref[:BLK, columns] = jnp.concatenate([first[:, :HEAD], second[:, :HEAD]], axis=1)
        rows_ref[BLK:, columns] = jnp.concatenate([first[:, HEAD:], second[:, HEAD:]], axis=1)
    mixed = jnp.dot(rows_ref[...], w_ref[...], preferred_element_type=jnp.float32)
    out_ref[...] = (x_ref[...].astype(jnp.float32) + mixed).astype(jnp.bfloat16)


def mix(attended, x, w):
    return pl.pallas_call(
        mix_kernel,
        out_shape=jax.ShapeDtypeStruct((ROWS, D), jnp.bfloat16),
        in_specs=[pl.BlockSpec(memory_space=pltpu.VMEM)] * 3,
        out_specs=pl.BlockSpec(memory_space=pltpu.VMEM),
        scratch_shapes=[pltpu.VMEM((ROWS, D), jnp.bfloat16)],
        compiler_params=pltpu.CompilerParams(vmem_limit_bytes=16 * 2**20),
        name="mix",
    )(in_vmem(attended), in_vmem(x), in_vmem(w))


def shards(series, block_time, w_qkv, w_out):
    sent = project(series, w_qkv)
    received = lax.all_to_all(sent, "tm", 0, 0, tiled=True)
    attended = attend(block_time, received)
    returned = lax.all_to_all(attended, "tm", 0, 0, tiled=True)
    return mix(returned, series, w_out)


def solution(mesh):
    placed = (P(("clus", "tm"), None), P("clus"), P(), P())
    return jax.shard_map(
        shards, mesh=mesh, in_specs=placed, out_specs=P(("clus", "tm"), None), check_vma=False
    )
```

```python
import jax
import jax.numpy as jnp
from jax import lax
from jax.experimental import pallas as pl
from jax.experimental.pallas import tpu as pltpu
from jax.sharding import PartitionSpec as P

HEADS = 16
HEAD = 64
D = 1024
BLK = 64
ROWS = 2 * BLK
N_TM = 16
TOKENS = N_TM * ROWS
QTILE = 512
KTILE = 1024
GROUP = 256
CHUNK = 256
PROJECT_VMEM = 24 * 2**20
NT = (((1,), (1,)), ((), ()))
SCALE = 0.125 * 1.4426950408889634


def in_hbm(array):
    return pltpu.with_memory_space_constraint(array, pltpu.HBM)


def in_vmem(array):
    return pltpu.with_memory_space_constraint(array, pltpu.VMEM)


def swap_halves(tile):
    top, low = tile[:BLK], tile[BLK:]
    first = jnp.concatenate([top[:, :HEAD], low[:, :HEAD]], axis=1)
    second = jnp.concatenate([top[:, HEAD:], low[:, HEAD:]], axis=1)
    return first, second


def project_kernel(x_ref, w_ref, time_ref, out_ref, time_out, x_buf, w_buf, total, sem):
    chunks = D // CHUNK
    x_copy = pltpu.make_async_copy(x_ref, x_buf, sem.at[chunks])
    x_copy.start()
    time_copy = pltpu.make_async_copy(time_ref, time_out, sem.at[chunks + 1])
    copies = []
    for c in range(chunks):
        rows = pl.ds(c * CHUNK, CHUNK)
        copies.append(pltpu.make_async_copy(w_ref.at[rows], w_buf.at[rows], sem.at[c]))
        copies[-1].start()
    time_copy.start()
    x_copy.wait()
    for c in range(chunks):
        copies[c].wait()
        depth = slice(c * CHUNK, (c + 1) * CHUNK)
        for g in range(3 * D // GROUP):
            columns = slice(g * GROUP, (g + 1) * GROUP)
            y = jnp.dot(
                x_buf[:, depth], w_buf[depth, columns], preferred_element_type=jnp.float32
            )
            if c:
                y = y + total[:, columns]
            if c < chunks - 1:
                total[:, columns] = y
                continue
            y = y.astype(jnp.bfloat16)
            part, start = g * GROUP // D, g * GROUP % D
            for pair in range(GROUP // 128):
                first, second = swap_halves(y[:, pair * 128 : pair * 128 + 128])
                head = start // HEAD + 2 * pair
                out_ref[head, part * BLK : part * BLK + BLK, :] = first
                out_ref[head + 1, part * BLK : part * BLK + BLK, :] = second
    time_copy.wait()


def project(x, w, block_time):
    return pl.pallas_call(
        project_kernel,
        out_shape=[
            pltpu.VMEM((HEADS, 3 * BLK, ROWS), jnp.bfloat16),
            pltpu.SMEM((2 * N_TM,), jnp.int32),
        ],
        in_specs=[pl.BlockSpec(memory_space=pl.ANY)] * 3,
        out_specs=[pl.BlockSpec(memory_space=pltpu.VMEM), pl.BlockSpec(memory_space=pltpu.SMEM)],
        scratch_shapes=[
            pltpu.VMEM((ROWS, D), jnp.bfloat16),
            pltpu.VMEM((D, 3 * D), jnp.bfloat16),
            pltpu.VMEM((ROWS, 3 * D), jnp.float32),
            pltpu.SemaphoreType.DMA((D // CHUNK + 2,)),
        ],
        compiler_params=pltpu.CompilerParams(vmem_limit_bytes=PROJECT_VMEM),
        name="project",
    )(in_hbm(x), in_hbm(w), in_hbm(block_time))


def attend_kernel(time_ref, in_ref, out_ref, qs, ks, vs, os):
    ones = jnp.ones((BLK, HEAD), jnp.bfloat16)
    for b in range(2 * N_TM):
        source, half = b // 2, b % 2
        rows = pl.ds(pl.multiple_of(time_ref[b] * BLK, BLK), BLK)
        columns = slice(half * HEAD, half * HEAD + HEAD)
        qs[rows, :] = in_ref[source, :BLK, columns]
        ks[rows, :] = in_ref[source, BLK : 2 * BLK, columns]
        vs[rows, :] = jnp.concatenate([in_ref[source, 2 * BLK :, columns], ones], axis=1)
    for start in range(0, TOKENS, QTILE):
        q = qs[start : start + QTILE, :]
        top = summed = None
        for first in range(0, start + QTILE, KTILE):
            last = min(first + KTILE, start + QTILE)
            scores = lax.dot_general(q, ks[first:last, :], NT, preferred_element_type=jnp.float32)
            if last > start:
                shape = (QTILE, last - first)
                later = lax.broadcasted_iota(jnp.int32, shape, 0) + start
                earlier = lax.broadcasted_iota(jnp.int32, shape, 1) + first
                scores = jnp.where(earlier <= later, scores, -1e30)
            new_top = jnp.max(scores, axis=1, keepdims=True)
            if top is not None:
                new_top = jnp.maximum(top, new_top)
            probs = jnp.exp2((scores - new_top) * SCALE).astype(jnp.bfloat16)
            added = jnp.dot(probs, vs[first:last, :], preferred_element_type=jnp.float32)
            if top is not None:
                added = summed * jnp.exp2((top - new_top) * SCALE) + added
            top, summed = new_top, added
        os[start : start + QTILE, :] = (summed[:, :HEAD] / summed[:, HEAD:]).astype(jnp.bfloat16)
    for s in range(N_TM):
        pair = []
        for half in range(2):
            rows = pl.ds(pl.multiple_of(time_ref[2 * s + half] * BLK, BLK), BLK)
            pair.append(os[rows, :])
        out_ref[s] = jnp.concatenate(pair, axis=1)


def attend(block_time, received):
    return pl.pallas_call(
        attend_kernel,
        out_shape=pltpu.VMEM((N_TM, BLK, ROWS), jnp.bfloat16),
        in_specs=[
            pl.BlockSpec(memory_space=pltpu.SMEM),
            pl.BlockSpec(memory_space=pltpu.VMEM),
        ],
        out_specs=pl.BlockSpec(memory_space=pltpu.VMEM),
        scratch_shapes=[
            pltpu.VMEM((TOKENS, HEAD), jnp.bfloat16),
            pltpu.VMEM((TOKENS, HEAD), jnp.bfloat16),
            pltpu.VMEM((TOKENS, 2 * HEAD), jnp.bfloat16),
            pltpu.VMEM((TOKENS, HEAD), jnp.bfloat16),
        ],
        compiler_params=pltpu.CompilerParams(vmem_limit_bytes=32 * 2**20),
        name="attend",
    )(pltpu.with_memory_space_constraint(block_time, pltpu.SMEM), in_vmem(received))


def mix_kernel(in_ref, x_ref, w_ref, out_ref, rows_ref):
    for pair in range(HEADS // 2):
        first, second = in_ref[2 * pair], in_ref[2 * pair + 1]
        columns = slice(pair * 128, pair * 128 + 128)
        rows_ref[:BLK, columns] = jnp.concatenate([first[:, :HEAD], second[:, :HEAD]], axis=1)
        rows_ref[BLK:, columns] = jnp.concatenate([first[:, HEAD:], second[:, HEAD:]], axis=1)
    mixed = jnp.dot(rows_ref[...], w_ref[...], preferred_element_type=jnp.float32)
    out_ref[...] = (x_ref[...].astype(jnp.float32) + mixed).astype(jnp.bfloat16)


def mix(attended, x, w):
    return pl.pallas_call(
        mix_kernel,
        out_shape=jax.ShapeDtypeStruct((ROWS, D), jnp.bfloat16),
        in_specs=[pl.BlockSpec(memory_space=pltpu.VMEM)] * 3,
        out_specs=pl.BlockSpec(memory_space=pltpu.VMEM),
        scratch_shapes=[pltpu.VMEM((ROWS, D), jnp.bfloat16)],
        compiler_params=pltpu.CompilerParams(vmem_limit_bytes=16 * 2**20),
        name="mix",
    )(in_vmem(attended), in_vmem(x), in_vmem(w))


def shards(series, block_time, w_qkv, w_out):
    sent, times = project(series, w_qkv, block_time)
    received = lax.all_to_all(sent, "tm", 0, 0, tiled=True)
    attended = attend(times, received)
    returned = lax.all_to_all(attended, "tm", 0, 0, tiled=True)
    return mix(returned, series, w_out)


def solution(mesh):
    placed = (P(("clus", "tm"), None), P("clus"), P(), P())
    return jax.shard_map(
        shards, mesh=mesh, in_specs=placed, out_specs=P(("clus", "tm"), None), check_vma=False
    )
```

```python
import jax
import jax.numpy as jnp
from jax import lax
from jax.experimental import pallas as pl
from jax.experimental.pallas import tpu as pltpu
from jax.sharding import PartitionSpec as P

HEADS = 16
HEAD = 64
D = 1024
BLK = 64
ROWS = 2 * BLK
N_TM = 16
TOKENS = N_TM * ROWS
QTILE = 512
KTILE = 1024
GROUP = 256
CHUNK = 256
PROJECT_VMEM = 24 * 2**20
NT = (((1,), (1,)), ((), ()))
SCALE = 0.125 * 1.4426950408889634


def in_hbm(array):
    return pltpu.with_memory_space_constraint(array, pltpu.HBM)


def in_vmem(array):
    return pltpu.with_memory_space_constraint(array, pltpu.VMEM)


def swap_halves(tile):
    top, low = tile[:BLK], tile[BLK:]
    first = jnp.concatenate([top[:, :HEAD], low[:, :HEAD]], axis=1)
    second = jnp.concatenate([top[:, HEAD:], low[:, HEAD:]], axis=1)
    return first, second


def project_kernel(x_ref, w_ref, time_ref, out_ref, time_out, x_buf, w_buf, total, sem):
    chunks = D // CHUNK
    x_copy = pltpu.make_async_copy(x_ref, x_buf, sem.at[chunks])
    x_copy.start()
    time_copy = pltpu.make_async_copy(time_ref, time_out, sem.at[chunks + 1])
    copies = []
    for c in range(chunks):
        rows = pl.ds(c * CHUNK, CHUNK)
        copies.append(pltpu.make_async_copy(w_ref.at[rows], w_buf.at[rows], sem.at[c]))
        copies[-1].start()
    time_copy.start()
    x_copy.wait()
    for c in range(chunks):
        copies[c].wait()
        depth = slice(c * CHUNK, (c + 1) * CHUNK)
        for g in range(D // GROUP):
            parts = []
            for part in range(3):
                columns = slice(part * D + g * GROUP, part * D + (g + 1) * GROUP)
                y = jnp.dot(
                    x_buf[:, depth], w_buf[depth, columns], preferred_element_type=jnp.float32
                )
                if c:
                    y = y + total[:, columns]
                if c < chunks - 1:
                    total[:, columns] = y
                parts.append(y.astype(jnp.bfloat16))
            if c < chunks - 1:
                continue
            for pair in range(GROUP // 128):
                q, k, v = (y[:, pair * 128 : pair * 128 + 128] for y in parts)
                head = g * GROUP // HEAD + 2 * pair
                first, second = swap_halves(k)
                out_ref[head, :ROWS, :] = jnp.concatenate([q[:, :HEAD], v[:, :HEAD]], axis=1)
                out_ref[head, ROWS:, :] = first
                out_ref[head + 1, :ROWS, :] = jnp.concatenate([q[:, HEAD:], v[:, HEAD:]], axis=1)
                out_ref[head + 1, ROWS:, :] = second
    time_copy.wait()


def project(x, w, block_time):
    return pl.pallas_call(
        project_kernel,
        out_shape=[
            pltpu.VMEM((HEADS, 3 * BLK, ROWS), jnp.bfloat16),
            pltpu.SMEM((2 * N_TM,), jnp.int32),
        ],
        in_specs=[pl.BlockSpec(memory_space=pl.ANY)] * 3,
        out_specs=[pl.BlockSpec(memory_space=pltpu.VMEM), pl.BlockSpec(memory_space=pltpu.SMEM)],
        scratch_shapes=[
            pltpu.VMEM((ROWS, D), jnp.bfloat16),
            pltpu.VMEM((D, 3 * D), jnp.bfloat16),
            pltpu.VMEM((ROWS, 3 * D), jnp.float32),
            pltpu.SemaphoreType.DMA((D // CHUNK + 2,)),
        ],
        compiler_params=pltpu.CompilerParams(vmem_limit_bytes=PROJECT_VMEM),
        name="project",
    )(in_hbm(x), in_hbm(w), in_hbm(block_time))


def attend_kernel(time_ref, in_ref, out_ref, qs, ks, vs, os):
    lower = lax.broadcasted_iota(jnp.int32, (BLK, ROWS), 1) < HEAD
    for b in range(2 * N_TM):
        source, half = b // 2, b % 2
        rows = pl.ds(pl.multiple_of(time_ref[b] * BLK, BLK), BLK)
        both = in_ref[source, half * BLK : half * BLK + BLK, :]
        keys = in_ref[source, ROWS:, :]
        if half:
            keys = jnp.concatenate([keys[:, HEAD:], keys[:, :HEAD]], axis=1)
        qs[rows, :] = jnp.where(lower, both, jnp.zeros_like(both))
        ks[rows, :] = keys
        vs[rows, :] = jnp.where(lower, jnp.ones_like(both), both)
    for start in range(0, TOKENS, QTILE):
        q = qs[start : start + QTILE, :]
        top = summed = None
        for first in range(0, start + QTILE, KTILE):
            last = min(first + KTILE, start + QTILE)
            scores = lax.dot_general(q, ks[first:last, :], NT, preferred_element_type=jnp.float32)
            if last > start:
                shape = (QTILE, last - first)
                later = lax.broadcasted_iota(jnp.int32, shape, 0) + start
                earlier = lax.broadcasted_iota(jnp.int32, shape, 1) + first
                scores = jnp.where(earlier <= later, scores, -1e30)
            new_top = jnp.max(scores, axis=1, keepdims=True)
            if top is not None:
                new_top = jnp.maximum(top, new_top)
            probs = jnp.exp2((scores - new_top) * SCALE).astype(jnp.bfloat16)
            added = jnp.dot(probs, vs[first:last, :], preferred_element_type=jnp.float32)
            if top is not None:
                added = summed * jnp.exp2((top - new_top) * SCALE) + added
            top, summed = new_top, added
        totals = jnp.concatenate([summed[:, HEAD:], summed[:, :HEAD]], axis=1)
        os[start : start + QTILE, :] = (summed / totals).astype(jnp.bfloat16)
    for s in range(N_TM):
        pair = []
        for half in range(2):
            rows = pl.ds(pl.multiple_of(time_ref[2 * s + half] * BLK, BLK), BLK)
            pair.append(os[rows, HEAD:])
        out_ref[s] = jnp.concatenate(pair, axis=1)


def attend(block_time, received):
    return pl.pallas_call(
        attend_kernel,
        out_shape=pltpu.VMEM((N_TM, BLK, ROWS), jnp.bfloat16),
        in_specs=[
            pl.BlockSpec(memory_space=pltpu.SMEM),
            pl.BlockSpec(memory_space=pltpu.VMEM),
        ],
        out_specs=pl.BlockSpec(memory_space=pltpu.VMEM),
        scratch_shapes=[
            pltpu.VMEM((TOKENS, 2 * HEAD), jnp.bfloat16),
            pltpu.VMEM((TOKENS, 2 * HEAD), jnp.bfloat16),
            pltpu.VMEM((TOKENS, 2 * HEAD), jnp.bfloat16),
            pltpu.VMEM((TOKENS, 2 * HEAD), jnp.bfloat16),
        ],
        compiler_params=pltpu.CompilerParams(vmem_limit_bytes=32 * 2**20),
        name="attend",
    )(pltpu.with_memory_space_constraint(block_time, pltpu.SMEM), in_vmem(received))


def mix_kernel(in_ref, x_ref, w_ref, out_ref, rows_ref):
    for pair in range(HEADS // 2):
        first, second = in_ref[2 * pair], in_ref[2 * pair + 1]
        columns = slice(pair * 128, pair * 128 + 128)
        rows_ref[:BLK, columns] = jnp.concatenate([first[:, :HEAD], second[:, :HEAD]], axis=1)
        rows_ref[BLK:, columns] = jnp.concatenate([first[:, HEAD:], second[:, HEAD:]], axis=1)
    mixed = jnp.dot(rows_ref[...], w_ref[...], preferred_element_type=jnp.float32)
    out_ref[...] = (x_ref[...].astype(jnp.float32) + mixed).astype(jnp.bfloat16)


def mix(attended, x, w):
    return pl.pallas_call(
        mix_kernel,
        out_shape=jax.ShapeDtypeStruct((ROWS, D), jnp.bfloat16),
        in_specs=[pl.BlockSpec(memory_space=pltpu.VMEM)] * 3,
        out_specs=pl.BlockSpec(memory_space=pltpu.VMEM),
        scratch_shapes=[pltpu.VMEM((ROWS, D), jnp.bfloat16)],
        compiler_params=pltpu.CompilerParams(vmem_limit_bytes=16 * 2**20),
        name="mix",
    )(in_vmem(attended), in_vmem(x), in_vmem(w))


def shards(series, block_time, w_qkv, w_out):
    sent, times = project(series, w_qkv, block_time)
    received = lax.all_to_all(sent, "tm", 0, 0, tiled=True)
    attended = attend(times, received)
    returned = lax.all_to_all(attended, "tm", 0, 0, tiled=True)
    return mix(returned, series, w_out)


def solution(mesh):
    placed = (P(("clus", "tm"), None), P("clus"), P(), P())
    return jax.shard_map(
        shards, mesh=mesh, in_specs=placed, out_specs=P(("clus", "tm"), None), check_vma=False
    )
```

```python
import jax
import jax.numpy as jnp
from jax import lax
from jax.experimental import pallas as pl
from jax.experimental.pallas import tpu as pltpu
from jax.sharding import PartitionSpec as P

HEADS = 16
HEAD = 64
D = 1024
BLK = 64
ROWS = 2 * BLK
N_TM = 16
TOKENS = N_TM * ROWS
QTILE = 512
KTILE = 1024
GROUP = 256
CHUNK = 128
PROJECT_VMEM = 24 * 2**20
NT = (((1,), (1,)), ((), ()))
SCALE = 0.125 * 1.4426950408889634


def in_hbm(array):
    return pltpu.with_memory_space_constraint(array, pltpu.HBM)


def in_vmem(array):
    return pltpu.with_memory_space_constraint(array, pltpu.VMEM)


def swap_halves(tile):
    top, low = tile[:BLK], tile[BLK:]
    first = jnp.concatenate([top[:, :HEAD], low[:, :HEAD]], axis=1)
    second = jnp.concatenate([top[:, HEAD:], low[:, HEAD:]], axis=1)
    return first, second


def project_kernel(x_ref, w_ref, time_ref, out_ref, time_out, x_buf, w_buf, total, sem):
    chunks = D // CHUNK
    x_copy = pltpu.make_async_copy(x_ref, x_buf, sem.at[chunks])
    x_copy.start()
    time_copy = pltpu.make_async_copy(time_ref, time_out, sem.at[chunks + 1])
    copies = []
    for c in range(chunks):
        rows = pl.ds(c * CHUNK, CHUNK)
        copies.append(pltpu.make_async_copy(w_ref.at[rows], w_buf.at[rows], sem.at[c]))
        copies[-1].start()
    time_copy.start()
    x_copy.wait()
    for c in range(chunks):
        copies[c].wait()
        depth = slice(c * CHUNK, (c + 1) * CHUNK)
        for g in range(3 * D // GROUP):
            columns = slice(g * GROUP, (g + 1) * GROUP)
            y = jnp.dot(
                x_buf[:, depth], w_buf[depth, columns], preferred_element_type=jnp.float32
            )
            if c:
                y = y + total[:, columns]
            if c < chunks - 1:
                total[:, columns] = y
                continue
            y = y.astype(jnp.bfloat16)
            part, start = g * GROUP // D, g * GROUP % D
            for pair in range(GROUP // 128):
                first, second = swap_halves(y[:, pair * 128 : pair * 128 + 128])
                head = start // HEAD + 2 * pair
                out_ref[head, part * BLK : part * BLK + BLK, :] = first
                out_ref[head + 1, part * BLK : part * BLK + BLK, :] = second
    time_copy.wait()


def project(x, w, block_time):
    return pl.pallas_call(
        project_kernel,
        out_shape=[
            pltpu.VMEM((HEADS, 3 * BLK, ROWS), jnp.bfloat16),
            pltpu.SMEM((2 * N_TM,), jnp.int32),
        ],
        in_specs=[pl.BlockSpec(memory_space=pl.ANY)] * 3,
        out_specs=[pl.BlockSpec(memory_space=pltpu.VMEM), pl.BlockSpec(memory_space=pltpu.SMEM)],
        scratch_shapes=[
            pltpu.VMEM((ROWS, D), jnp.bfloat16),
            pltpu.VMEM((D, 3 * D), jnp.bfloat16),
            pltpu.VMEM((ROWS, 3 * D), jnp.float32),
            pltpu.SemaphoreType.DMA((D // CHUNK + 2,)),
        ],
        compiler_params=pltpu.CompilerParams(vmem_limit_bytes=PROJECT_VMEM),
        name="project",
    )(in_hbm(x), in_hbm(w), in_hbm(block_time))


def attend_kernel(time_ref, in_ref, out_ref, qs, ks, vs, os):
    ones = jnp.ones((BLK, HEAD), jnp.bfloat16)
    for b in range(2 * N_TM):
        source, half = b // 2, b % 2
        rows = pl.ds(pl.multiple_of(time_ref[b] * BLK, BLK), BLK)
        columns = slice(half * HEAD, half * HEAD + HEAD)
        qs[rows, :] = in_ref[source, :BLK, columns]
        ks[rows, :] = in_ref[source, BLK : 2 * BLK, columns]
        vs[rows, :] = jnp.concatenate([in_ref[source, 2 * BLK :, columns], ones], axis=1)
    for start in range(0, TOKENS, QTILE):
        q = qs[start : start + QTILE, :]
        top = summed = None
        for first in range(0, start + QTILE, KTILE):
            last = min(first + KTILE, start + QTILE)
            scores = lax.dot_general(q, ks[first:last, :], NT, preferred_element_type=jnp.float32)
            if last > start:
                shape = (QTILE, last - first)
                later = lax.broadcasted_iota(jnp.int32, shape, 0) + start
                earlier = lax.broadcasted_iota(jnp.int32, shape, 1) + first
                scores = jnp.where(earlier <= later, scores, -1e30)
            new_top = jnp.max(scores, axis=1, keepdims=True)
            if top is not None:
                new_top = jnp.maximum(top, new_top)
            probs = jnp.exp2((scores - new_top) * SCALE).astype(jnp.bfloat16)
            added = jnp.dot(probs, vs[first:last, :], preferred_element_type=jnp.float32)
            if top is not None:
                added = summed * jnp.exp2((top - new_top) * SCALE) + added
            top, summed = new_top, added
        os[start : start + QTILE, :] = (summed[:, :HEAD] / summed[:, HEAD:]).astype(jnp.bfloat16)
    for s in range(N_TM):
        pair = []
        for half in range(2):
            rows = pl.ds(pl.multiple_of(time_ref[2 * s + half] * BLK, BLK), BLK)
            pair.append(os[rows, :])
        out_ref[s] = jnp.concatenate(pair, axis=1)


def attend(block_time, received):
    return pl.pallas_call(
        attend_kernel,
        out_shape=pltpu.VMEM((N_TM, BLK, ROWS), jnp.bfloat16),
        in_specs=[
            pl.BlockSpec(memory_space=pltpu.SMEM),
            pl.BlockSpec(memory_space=pltpu.VMEM),
        ],
        out_specs=pl.BlockSpec(memory_space=pltpu.VMEM),
        scratch_shapes=[
            pltpu.VMEM((TOKENS, HEAD), jnp.bfloat16),
            pltpu.VMEM((TOKENS, HEAD), jnp.bfloat16),
            pltpu.VMEM((TOKENS, 2 * HEAD), jnp.bfloat16),
            pltpu.VMEM((TOKENS, HEAD), jnp.bfloat16),
        ],
        compiler_params=pltpu.CompilerParams(vmem_limit_bytes=32 * 2**20),
        name="attend",
    )(pltpu.with_memory_space_constraint(block_time, pltpu.SMEM), in_vmem(received))


def mix_kernel(in_ref, x_ref, w_ref, out_ref, rows_ref):
    for pair in range(HEADS // 2):
        first, second = in_ref[2 * pair], in_ref[2 * pair + 1]
        columns = slice(pair * 128, pair * 128 + 128)
        rows_ref[:BLK, columns] = jnp.concatenate([first[:, :HEAD], second[:, :HEAD]], axis=1)
        rows_ref[BLK:, columns] = jnp.concatenate([first[:, HEAD:], second[:, HEAD:]], axis=1)
    mixed = jnp.dot(rows_ref[...], w_ref[...], preferred_element_type=jnp.float32)
    out_ref[...] = (x_ref[...].astype(jnp.float32) + mixed).astype(jnp.bfloat16)


def mix(attended, x, w):
    return pl.pallas_call(
        mix_kernel,
        out_shape=jax.ShapeDtypeStruct((ROWS, D), jnp.bfloat16),
        in_specs=[pl.BlockSpec(memory_space=pltpu.VMEM)] * 3,
        out_specs=pl.BlockSpec(memory_space=pltpu.VMEM),
        scratch_shapes=[pltpu.VMEM((ROWS, D), jnp.bfloat16)],
        compiler_params=pltpu.CompilerParams(vmem_limit_bytes=16 * 2**20),
        name="mix",
    )(in_vmem(attended), in_vmem(x), in_vmem(w))


def shards(series, block_time, w_qkv, w_out):
    sent, times = project(series, w_qkv, block_time)
    received = lax.all_to_all(sent, "tm", 0, 0, tiled=True)
    attended = attend(times, received)
    returned = lax.all_to_all(attended, "tm", 0, 0, tiled=True)
    return mix(returned, series, w_out)


def solution(mesh):
    placed = (P(("clus", "tm"), None), P("clus"), P(), P())
    return jax.shard_map(
        shards, mesh=mesh, in_specs=placed, out_specs=P(("clus", "tm"), None), check_vma=False
    )
```
